256 devices in a mesh: section: 32 (over z, x_lo, core), tensor: 8 (over y, x_hi).
Axes of the slice: x: 4 (x_hi: 2, x_lo: 2; x = x_hi * 2 + x_lo), y: 4, z: 8, core: 2. Of those that a mesh axis runs over, the one named last changes fastest.
Arguments:
- saved_inputs: bfloat16 [32, 8, 256, 512], P('section', None, 'tensor'), may hold values from -6 to 6
- microbatch_slot: int32 [32, 3], P('section'), may hold values from 0 to 7
- staleness: int32 [32, 2], P('section'), may hold values from 1 to 2
- up_weight: bfloat16 [32, 512, 32768], P('section', None, 'tensor'), may hold values from -0.25 to 0.25
- down_weight: bfloat16 [32, 32768, 512], P('section', 'tensor'), may hold values from -0.03125 to 0.03125
- upstream_grad: bfloat16 [32, 256, 512], P('section', 'tensor'), may hold values from -6 to 6
- head_grad: bfloat16 [2, 256, 512], P(None, 'tensor'), may hold values from -6 to 6
Outputs:
- back_grad: bfloat16 [3, 32, 256, 512], P(None, 'section', 'tensor')
The draws below stay inside these ranges and needn't reach their ends.
All inputs are finite; a program needn't handle non-finite values.
Results may differ from the reference program's by a relative error of at most 0.025.
The reference program's roundings to bfloat16 on the way count: a program that leaves them out, or rounds other values in their place, can miss the bound.
Values may be sent and summed in bfloat16 or wider, within the bound.
No kernel may reach another device: no remote copies, remote signals or barrier semaphores. Data moves between devices by JAX's collectives and lax.ppermute only.
A program may use at most 128 MiB of HBM per device.

```python
import math
import jax
import jax.numpy as jnp
from jax import lax

D = 512
FF = 32768
ROWS = 256
SLOTS = 8
TICKS = 3
SECTIONS = 32


def touch_ends(drawn, own_key, smallest, high):
    index_at = [jax.random.randint(jax.random.fold_in(own_key, axis), (), 0, length) for axis, length in enumerate(drawn.shape)]
    main_axis = drawn.shape.index(max(drawn.shape))
    beside = index_at[:main_axis] + [(index_at[main_axis] + 1) % drawn.shape[main_axis]] + index_at[main_axis + 1:]
    return drawn.at[tuple(index_at)].set(smallest).at[tuple(beside)].set(high)


def level_of(own_key, extent, cuts, low, high):
    def one(axis_at, shards_of):
        steps = jax.random.uniform(jax.random.fold_in(jax.random.fold_in(own_key, 6), axis_at), (shards_of,), jnp.float32, low / len(cuts), high / len(cuts))
        return jnp.repeat(jnp.exp(steps), extent[axis_at] // shards_of).reshape((-1,) + (1,) * (len(extent) - axis_at - 1))

    gain = one(*cuts[0])
    for cut in cuts[1:]:
        gain = gain * one(*cut)
    return gain


def centred(rng, shape, scale, limit, cuts=(), dtype=jnp.bfloat16):
    level = level_of(rng, shape, cuts, -0.22, 0.18) if cuts else 1.0
    result = jax.random.normal(rng, shape, jnp.float32) * scale * level
    return jnp.minimum(jnp.maximum(result, -limit), limit).astype(dtype)


def setup_inputs(seed: int = 0) -> dict:
    key_of = jax.random.split(jax.random.key(seed), 8)
    saved_inputs = centred(key_of[0], (SECTIONS, SLOTS, ROWS, D), 1.0, 6.0, ((0, 32), (2, 8)))
    microbatch_slot = touch_ends(jax.random.randint(key_of[1], (SECTIONS, TICKS), 0, SLOTS), jax.random.fold_in(key_of[1], 1), 0, SLOTS - 1).astype(jnp.int32)
    staleness = touch_ends(jax.random.randint(key_of[2], (SECTIONS, TICKS - 1), 1, 3), jax.random.fold_in(key_of[2], 1), 1, 2).astype(jnp.int32)
    up_weight = centred(key_of[3], (SECTIONS, D, FF), D ** -0.5, 0.25, ((0, 32), (2, 8)))
    down_weight = centred(key_of[4], (SECTIONS, FF, D), FF ** -0.5, 0.03125, ((0, 32), (1, 8)))
    upstream_grad = centred(key_of[5], (SECTIONS, ROWS, D), 1.0, 6.0, ((0, 32), (1, 8)))
    head_grad = centred(key_of[6], (TICKS - 1, ROWS, D), 1.0, 6.0, ((1, 8),))
    return dict(saved_inputs=saved_inputs, microbatch_slot=microbatch_slot, staleness=staleness, up_weight=up_weight, down_weight=down_weight, upstream_grad=upstream_grad, head_grad=head_grad)


def learning_rates(total_rows, width, hidden_units):
    up_rate = 0.5 * math.sqrt(hidden_units) / (math.sqrt(total_rows) * width)
    down_rate = 0.5 / (math.sqrt(total_rows) * math.sqrt(hidden_units))
    return (up_rate, down_rate)

def weights_at(tick_index, weight_up, weight_down, gradients, delay_row, rates):
    if tick_index == 0:
        return (weight_up, weight_down)
    total_up = None
    total_down = None
    for earlier in range(tick_index):
        flag = (earlier + delay_row[earlier] <= tick_index).astype(jnp.float32)
        term_up = flag * gradients[earlier][0]
        term_down = flag * gradients[earlier][1]
        total_up = term_up if total_up is None else total_up + term_up
        total_down = term_down if total_down is None else total_down + term_down
    new_up = (weight_up.astype(jnp.float32) - rates[0] * total_up).astype(jnp.bfloat16)
    new_down = (weight_down.astype(jnp.float32) - rates[1] * total_down).astype(jnp.bfloat16)
    return (new_up, new_down)

def section_ticks(incoming, per_section):
    saved, chosen_slots, delay_row, weight_up, weight_down, first_grad = per_section
    rates = learning_rates(saved.shape[1], weight_up.shape[0], weight_up.shape[1])
    grad_out = first_grad
    gradients = []
    outputs = []
    for tick_index in range(TICKS):
        cur_up, cur_down = weights_at(tick_index, weight_up, weight_down, gradients, delay_row, rates)
        inputs = lax.dynamic_index_in_dim(saved, chosen_slots[tick_index], 0, keepdims=False)
        before_relu = jnp.dot(inputs, cur_up, preferred_element_type=jnp.float32)
        hidden_raw = lax.dot_general(grad_out, cur_down, (((1,), (1,)), ((), ())), preferred_element_type=jnp.float32)
        masked = jnp.where(before_relu > 0, hidden_raw, 0.0).astype(jnp.bfloat16)
        back = lax.dot_general(masked, cur_up, (((1,), (1,)), ((), ())), preferred_element_type=jnp.float32)
        outputs.append(back.astype(jnp.bfloat16))
        if tick_index + 1 < TICKS:
            hidden = jnp.maximum(before_relu, 0.0).astype(jnp.bfloat16)
            grad_up = lax.dot_general(inputs, masked, (((0,), (0,)), ((), ())), preferred_element_type=jnp.float32)
            grad_down = lax.dot_general(hidden, grad_out, (((0,), (0,)), ((), ())), preferred_element_type=jnp.float32)
            gradients.append((grad_up, grad_down))
            grad_out = incoming[tick_index]
    stacked = jnp.stack(outputs)
    return (stacked[:TICKS - 1], stacked)

def reference(saved_inputs, microbatch_slot, staleness, up_weight, down_weight, upstream_grad, head_grad):
    _, every = lax.scan(section_ticks, head_grad, (saved_inputs, microbatch_slot, staleness, up_weight, down_weight, upstream_grad), reverse=True)
    return jnp.transpose(every, (1, 0, 2, 3))
```

```python
import math

import jax
import jax.numpy as jnp
from jax import lax
from jax.sharding import PartitionSpec as P

F32 = jnp.float32
BF16 = jnp.bfloat16


def learning_rates(total_rows, width, hidden_units):
    up_rate = 0.5 * math.sqrt(hidden_units) / (math.sqrt(total_rows) * width)
    down_rate = 0.5 / (math.sqrt(total_rows) * math.sqrt(hidden_units))
    return (up_rate, down_rate)


def across_x(value):
    return lax.ppermute(value, "tensor", [(i, i ^ 1) for i in range(8)])


def along_y(value, by):
    return lax.ppermute(value, "tensor", [(i, (i + 2 * by) % 8) for i in range(8)])


def to_previous_section(value, flip):
    sections = lax.axis_size("section")
    pairs = [
        (s * 8 + i, (s - 1) * 8 + (i ^ flip)) for s in range(1, sections) for i in range(8)
    ]
    return lax.ppermute(value, ("section", "tensor"), pairs)


def pair_rows(rows):
    return jnp.concatenate([rows, across_x(rows)], axis=1)


def gather_blocks(block, axis):
    return jnp.concatenate([block] + [along_y(block, -by) for by in (1, 2, 3)], axis=axis)


def sum_along_y(partial):
    rounded = partial.astype(BF16)
    total = partial[:64]
    for by in (1, 2, 3):
        total = total + along_y(rounded[64 * by : 64 * by + 64], by).astype(F32)
    return total


def swapped(block):
    return jnp.concatenate([block[32:], block[:32]], axis=0)


def dot(a, b, dims):
    return lax.dot_general(a, b, (dims, ((), ())), preferred_element_type=F32)


def body(
    saved_inputs, microbatch_slot, staleness, up_weight, down_weight, upstream_grad, head_grad
):
    is_last = lax.axis_index("section") == lax.axis_size("section") - 1
    first_up = up_weight[0]
    first_down = down_weight[0]
    slots = microbatch_slot[0]
    delay = staleness[0]
    rates = learning_rates(256, first_up.shape[0], first_up.shape[1] * 8)

    def input_rows(tick):
        return lax.dynamic_index_in_dim(saved_inputs[0], slots[tick], 0, keepdims=False)

    def flag(tick, earlier):
        return (earlier + delay[earlier] <= tick).astype(F32)

    gathered = gather_blocks(pair_rows(jnp.stack([upstream_grad[0], input_rows(0)])), 1)
    grad, inputs = gathered[0], gathered[1]
    pairs = pair_rows(
        jnp.concatenate([jnp.stack([input_rows(1), input_rows(2)]), head_grad], axis=0)
    )
    later = gather_blocks(pairs[:2], 1)
    all_inputs = [inputs, later[0], later[1]]
    head = [pairs[2], pairs[3]]

    up, down = first_up, first_down
    hiddens, maskeds, grads = [], [], []
    own, sent = [], []
    for tick in range(3):
        inputs = all_inputs[tick]
        before = dot(inputs, up, ((1,), (0,)))
        raw = dot(grad, down, ((1,), (1,)))
        masked = jnp.where(before > 0, raw, 0.0).astype(BF16)
        partial = dot(masked, up, ((1,), (1,)))
        total = sum_along_y(partial)
        own.append(total[:32])
        sent.append(total[32:].astype(BF16))
        if tick < 2:
            hiddens.append(jnp.maximum(before, 0.0).astype(BF16))
            maskeds.append(masked)
            grads.append(grad)
            rounded = total.astype(BF16)
            arrived = to_previous_section(rounded, 0).astype(F32) + to_previous_section(
                swapped(rounded), 1
            ).astype(F32)
            flags = [flag(tick + 1, j).astype(BF16) for j in range(tick + 1)]
            scaled_inputs = jnp.concatenate(
                [f * x for f, x in zip(flags, all_inputs)], axis=0
            )
            scaled_grads = jnp.concatenate([f * g for f, g in zip(flags, grads)], axis=0)
            all_masked = jnp.concatenate(maskeds, axis=0)
            all_hidden = jnp.concatenate(hiddens, axis=0)
            up = (
                first_up.astype(F32) - rates[0] * dot(scaled_inputs, all_masked, ((0,), (0,)))
            ).astype(BF16)
            down = (
                first_down.astype(F32) - rates[1] * dot(all_hidden, scaled_grads, ((0,), (0,)))
            ).astype(BF16)
            grad = gather_blocks(jnp.where(is_last, head[tick], arrived.astype(BF16)), 0)
    out = jnp.stack(own) + across_x(jnp.stack(sent)).astype(F32)
    return out.astype(BF16)[:, None]


def solution(mesh):
    placed = (
        P("section", None, "tensor", None),
        P("section", None),
        P("section", None),
        P("section", None, "tensor"),
        P("section", "tensor", None),
        P("section", "tensor", None),
        P(None, "tensor", None),
    )
    return jax.shard_map(
        body,
        mesh=mesh,
        in_specs=placed,
        out_specs=P(None, "section", "tensor", None),
        check_vma=False,
    )
```

```python
import functools
import math

import jax
import jax.numpy as jnp
from jax import lax
from jax.experimental import pallas as pl
from jax.experimental.pallas import tpu as pltpu
from jax.sharding import PartitionSpec as P

F32 = jnp.float32
BF16 = jnp.bfloat16
CHUNK = 512
WIDE = 2048
PART = 2048
PARTS = 4096 // PART


def learning_rates(total_rows, width, hidden_units):
    up_rate = 0.5 * math.sqrt(hidden_units) / (math.sqrt(total_rows) * width)
    down_rate = 0.5 / (math.sqrt(total_rows) * math.sqrt(hidden_units))
    return (up_rate, down_rate)


def across_x(value):
    return lax.ppermute(value, "tensor", [(i, i ^ 1) for i in range(8)])


def along_y(value, by):
    return lax.ppermute(value, "tensor", [(i, (i + 2 * by) % 8) for i in range(8)])


def to_previous_section(value, flip):
    sections = lax.axis_size("section")
    pairs = [
        (s * 8 + i, (s - 1) % sections * 8 + (i ^ flip))
        for s in range(sections)
        for i in range(8)
    ]
    return lax.ppermute(value, ("section", "tensor"), pairs)


def pair_rows(rows):
    return jnp.concatenate([rows, across_x(rows)], axis=1)


def gather_blocks(block, axis):
    return jnp.concatenate([block] + [along_y(block, -by) for by in (1, 2, 3)], axis=axis)


def swapped(block):
    return jnp.concatenate([block[32:], block[:32]], axis=0)


def dot(a, b, dims):
    return lax.dot_general(a, b, (dims, ((), ())), preferred_element_type=F32)


IN_VMEM = pl.BlockSpec(memory_space=pltpu.VMEM)
IN_SMEM = pl.BlockSpec(memory_space=pltpu.SMEM)
IN_HBM = pl.BlockSpec(memory_space=pl.ANY)


def held(value):
    return pltpu.with_memory_space_constraint(value, pltpu.VMEM)


def left(value):
    return pltpu.with_memory_space_constraint(value, pltpu.HBM)


def call(kernel, outs, specs, matmuls, name, *operands, scratch=()):
    place = {id(IN_VMEM): held, id(IN_HBM): left}
    operands = [place.get(id(s), lambda x: x)(x) for x, s in zip(operands, specs)]
    return pl.pallas_call(
        kernel,
        out_shape=tuple(pltpu.VMEM(shape, dtype) for shape, dtype in outs),
        in_specs=list(specs),
        out_specs=(IN_VMEM,) * len(outs),
        scratch_shapes=list(scratch),
        compiler_params=pltpu.CompilerParams(vmem_limit_bytes=10 << 20),
        cost_estimate=pl.CostEstimate(
            flops=int(matmuls * 2 * 256 * 512 * 4096), bytes_accessed=0, transcendentals=0
        ),
        name=name,
    )(*operands)


def pick_kernel(slots, saved, upstream, head, now, later, slot_values, sems):
    slot_copy = pltpu.make_async_copy(slots, slot_values, sems.at[6])
    copies = [
        pltpu.make_async_copy(upstream.at[0], now.at[0], sems.at[0]),
        pltpu.make_async_copy(head.at[0], later.at[2], sems.at[1]),
        pltpu.make_async_copy(head.at[1], later.at[3], sems.at[2]),
    ]
    slot_copy.start()
    for copy in copies:
        copy.start()
    slot_copy.wait()
    for tick, place in enumerate((now.at[1], later.at[0], later.at[1])):
        slot = jnp.clip(slot_values[0, tick], 0, 7)
        copies.append(pltpu.make_async_copy(saved.at[0, slot], place, sems.at[3 + tick]))
        copies[-1].start()
    for copy in copies:
        copy.wait()


LOADS = 4


def load_kernel(after, up, down, held_up, held_down, sems):
    copies = []
    for i in range(LOADS):
        rows = pl.ds(i * (512 // LOADS), 512 // LOADS)
        copies.append(pltpu.make_async_copy(up.at[0, rows], held_up.at[rows], sems.at[2 * i]))
        rows = pl.ds(i * (4096 // LOADS), 4096 // LOADS)
        copies.append(
            pltpu.make_async_copy(down.at[0, rows], held_down.at[rows], sems.at[2 * i + 1])
        )
    for copy in copies:
        copy.start()
    for copy in copies:
        copy.wait()


def emit(total, own, others):
    own[...] = total[:64]
    for by, other in enumerate(others):
        other[...] = total[64 * by + 64 : 64 * by + 128].astype(BF16)


def emit_chunks(total, chunks):
    index = lax.axis_index("tensor")
    y, x_hi = lax.div(index, 2), lax.rem(index, 2)
    for by in range(4):
        for other in range(2):
            owner = 2 * lax.rem(y + by, 4) + lax.rem(x_hi + other, 2)
            at = 64 * by + 32 * other
            chunks[owner] = total[at : at + 32].astype(BF16)


PARTIAL = [((64, 512), F32)] + [((64, 512), BF16)] * 3
HIDDEN = [((256, PART), BF16)] * PARTS


def first_kernel(inputs, grad, up, down, own, o1, o2, o3, *refs):
    hiddens, maskeds = refs[:PARTS], refs[PARTS:]
    total = None
    for i in range(PARTS):
        for at in range(0, PART, WIDE):
            here = slice(at, at + WIDE)
            part = slice(i * PART + at, i * PART + at + WIDE)
            before = dot(inputs[...], up[:, part], ((1,), (0,)))
            hiddens[i][:, here] = jnp.maximum(before, 0.0).astype(BF16)
            raw = dot(grad[...], down[part, :], ((1,), (1,)))
            value = jnp.where(before > 0, raw, 0.0).astype(BF16)
            maskeds[i][:, here] = value
            term = dot(value, up[:, part], ((1,), (1,)))
            total = term if total is None else total + term
    emit(total, own, (o1, o2, o3))


def next_kernel(grad, *refs):
    hiddens, ups, downs = (refs[i * PARTS : (i + 1) * PARTS] for i in range(3))
    outs = refs[3 * PARTS :]
    masked = outs[4:]
    total = None
    for i in range(PARTS):
        for at in range(0, PART, WIDE):
            part = slice(at, at + WIDE)
            raw = dot(grad[...], downs[i][part, :], ((1,), (1,)))
            value = jnp.where(hiddens[i][:, part] > 0, raw, 0.0).astype(BF16)
            if masked:
                masked[i][:, part] = value
            term = dot(value, ups[i][:, part], ((1,), (1,)))
            total = term if total is None else total + term
    if masked:
        emit(total, outs[0], outs[1:4])
    else:
        emit_chunks(total, outs[0])


def flags_at(delay, tick):
    return [(j + delay[0, j] <= tick).astype(F32) for j in range(tick)]


def up_kernel(tick, part_at, rate, given, delay, *refs):
    inputs, maskeds = refs[:tick], refs[tick : 2 * tick]
    following, first_up = refs[2 * tick : 2 * tick + 2]
    totals = refs[2 * tick + 2 : 2 * tick + 2 + given]
    up, hidden, *sent = refs[2 * tick + 2 + given :]
    if sent:
        for at, total in enumerate(totals):
            sent[0][at] = total[32:64].astype(BF16)
    flags = flags_at(delay, tick)
    turned = jnp.concatenate(
        [(flag * x[...].astype(F32)).astype(BF16) for flag, x in zip(flags, inputs)], axis=0
    ).T
    for at in range(0, PART, CHUNK):
        part = slice(part_at + at, part_at + at + CHUNK)
        here = slice(at, at + CHUNK)
        masked = jnp.concatenate([m[:, here] for m in maskeds], axis=0)
        total = dot(turned, masked, ((1,), (0,)))
        value = (first_up[0, :, part].astype(F32) - rate * total).astype(BF16)
        up[:, here] = value
        before = dot(following[...], value, ((1,), (0,)))
        hidden[:, here] = jnp.maximum(before, 0.0).astype(BF16)


def down_kernel(tick, part_at, rate, delay, *refs):
    hiddens, grads = refs[:tick], refs[tick : 2 * tick]
    first_down, given, down, *passed = refs[2 * tick :]
    if passed:
        passed[0][...] = given[...]
    flags = flags_at(delay, tick)
    scaled = jnp.concatenate(
        [(flag * g[...].astype(F32)).astype(BF16) for flag, g in zip(flags, grads)], axis=0
    )
    for at in range(0, PART, CHUNK):
        part = slice(part_at + at, part_at + at + CHUNK)
        here = slice(at, at + CHUNK)
        hidden = jnp.concatenate([h[:, here] for h in hiddens], axis=0)
        total = dot(hidden, scaled, ((0,), (0,)))
        down[here, :] = (first_down[0, part, :].astype(F32) - rate * total).astype(BF16)


def body(
    saved_inputs, microbatch_slot, staleness, up_weight, down_weight, upstream_grad, head_grad
):
    is_last = lax.axis_index("section") == lax.axis_size("section") - 1
    rates = learning_rates(256, 512, 32768)

    now, later = call(
        pick_kernel,
        [((2, 32, 512), BF16), ((4, 32, 512), BF16)],
        (IN_HBM,) * 4,
        0,
        "pick",
        microbatch_slot,
        saved_inputs,
        upstream_grad,
        head_grad,
        scratch=(pltpu.SMEM((1, 3), jnp.int32), pltpu.SemaphoreType.DMA((7,))),
    )
    now_pairs = pair_rows(now)
    first_up, first_down = call(
        load_kernel,
        [((512, 4096), BF16), ((4096, 512), BF16)],
        (IN_VMEM, IN_HBM, IN_HBM),
        2,
        "load",
        now_pairs,
        up_weight,
        down_weight,
        scratch=(pltpu.SemaphoreType.DMA((2 * LOADS,)),),
    )
    gathered = gather_blocks(now_pairs, 1)
    grad = gathered[0]
    inputs = [gathered[1]]
    pairs = pair_rows(later)
    head = [pairs[2], pairs[3]]

    hiddens, maskeds, grads, totals = [], [], [], []
    for tick in range(3):
        if tick == 0:
            outs = call(
                first_kernel,
                PARTIAL + HIDDEN * 2,
                (IN_VMEM,) * 4,
                3,
                "first",
                inputs[0],
                grad,
                first_up,
                first_down,
            )
            hiddens.append(outs[4 : 4 + PARTS])
            maskeds.append(outs[4 + PARTS :])
        else:
            outs = call(
                next_kernel,
                PARTIAL + HIDDEN if tick < 2 else [((8, 32, 512), BF16)],
                (IN_VMEM,) * (1 + 3 * PARTS),
                2,
                "next",
                grad,
                *hiddens[tick],
                *ups,
                *downs,
            )
            maskeds.append(outs[4:])
        if tick == 2:
            chunks = lax.all_to_all(outs[0], "tensor", 0, 0)
            results.append(jnp.sum(chunks.astype(F32), axis=0).astype(BF16))
        else:
            grads.append(grad)
            total = outs[0]
            for by in (1, 2, 3):
                total = total + along_y(outs[by], by).astype(F32)
            totals.append(total)
            rounded = total.astype(BF16)
            arrived = to_previous_section(rounded, 0).astype(F32) + to_previous_section(
                swapped(rounded), 1
            ).astype(F32)
            done = tick + 1
            downs, both = [], []
            for i in range(PARTS):
                handed_on = tick == 0 and i == 0
                down, *passed = call(
                    functools.partial(down_kernel, done, i * PART, rates[1]),
                    [((PART, 512), BF16)] + [((2, 64, 512), BF16)] * handed_on,
                    (IN_SMEM,) + (IN_VMEM,) * (2 * done + 2),
                    done / PARTS,
                    "down",
                    staleness,
                    *[h[i] for h in hiddens],
                    *grads,
                    down_weight,
                    pairs[:2] if handed_on else rounded,
                )
                downs.append(down)
                if handed_on:
                    following = gather_blocks(passed[0], 1)
                    inputs += [following[0], following[1]]
            for i in range(PARTS):
                given = totals if i else []
                sends = tick == 1 and i == 1
                both.append(
                    call(
                        functools.partial(up_kernel, done, i * PART, rates[0], len(given)),
                        [((512, PART), BF16), ((256, PART), BF16)]
                        + [((2, 32, 512), BF16)] * sends,
                        (IN_SMEM,) + (IN_VMEM,) * (2 * done + 2 + len(given)),
                        (done + 1) / PARTS,
                        "up",
                        staleness,
                        *inputs[:done],
                        *[m[i] for m in maskeds],
                        inputs[done],
                        up_weight,
                        *given,
                    )
                )
            if tick == 1:
                others = across_x(both[1][2]).astype(F32)
                results = [
                    (total[:32] + others[t]).astype(BF16) for t, total in enumerate(totals)
                ]
            ups = [b[0] for b in both]
            hiddens.append([b[1] for b in both])
            grad = gather_blocks(jnp.where(is_last, head[tick], arrived.astype(BF16)), 0)
    return jnp.stack(results)[:, None]


def solution(mesh):
    placed = (
        P("section", None, "tensor", None),
        P("section", None),
        P("section", None),
        P("section", None, "tensor"),
        P("section", "tensor", None),
        P("section", "tensor", None),
        P(None, "tensor", None),
    )
    return jax.shard_map(
        body,
        mesh=mesh,
        in_specs=placed,
        out_specs=P(None, "section", "tensor", None),
        check_vma=False,
    )
```

```python
import functools
import math

import jax
import jax.numpy as jnp
from jax import lax
from jax.experimental import pallas as pl
from jax.experimental.pallas import tpu as pltpu
from jax.sharding import PartitionSpec as P

F32 = jnp.float32
BF16 = jnp.bfloat16
CHUNK = 512
WIDE = 1024
PART = 2048
PARTS = 4096 // PART


def learning_rates(total_rows, width, hidden_units):
    up_rate = 0.5 * math.sqrt(hidden_units) / (math.sqrt(total_rows) * width)
    down_rate = 0.5 / (math.sqrt(total_rows) * math.sqrt(hidden_units))
    return (up_rate, down_rate)


def across_x(value):
    return lax.ppermute(value, "tensor", [(i, i ^ 1) for i in range(8)])


def along_y(value, by):
    return lax.ppermute(value, "tensor", [(i, i ^ (2 * by)) for i in range(8)])


def to_previous_section(value, flip):
    sections = lax.axis_size("section")
    pairs = [
        (s * 8 + i, (s - 1) % sections * 8 + (i ^ flip))
        for s in range(sections)
        for i in range(8)
    ]
    return lax.ppermute(value, ("section", "tensor"), pairs)


def pair_rows(rows):
    return jnp.concatenate([rows, across_x(rows)], axis=1)


def gather_blocks(block, axis):
    return jnp.concatenate([block] + [along_y(block, by) for by in (1, 2, 3)], axis=axis)


def dot(a, b, dims):
    return lax.dot_general(a, b, (dims, ((), ())), preferred_element_type=F32)


IN_VMEM = pl.BlockSpec(memory_space=pltpu.VMEM)
IN_SMEM = pl.BlockSpec(memory_space=pltpu.SMEM)
IN_HBM = pl.BlockSpec(memory_space=pl.ANY)


def held(value):
    return pltpu.with_memory_space_constraint(value, pltpu.VMEM)


def left(value):
    return pltpu.with_memory_space_constraint(value, pltpu.HBM)


def call(kernel, outs, specs, matmuls, name, *operands, scratch=()):
    place = {id(IN_VMEM): held, id(IN_HBM): left}
    operands = [place.get(id(s), lambda x: x)(x) for x, s in zip(operands, specs)]
    return pl.pallas_call(
        kernel,
        out_shape=tuple(pltpu.VMEM(shape, dtype) for shape, dtype in outs),
        in_specs=list(specs),
        out_specs=(IN_VMEM,) * len(outs),
        scratch_shapes=list(scratch),
        compiler_params=pltpu.CompilerParams(vmem_limit_bytes=10 << 20),
        cost_estimate=pl.CostEstimate(
            flops=int(matmuls * 2 * 256 * 512 * 4096), bytes_accessed=0, transcendentals=0
        ),
        name=name,
    )(*operands)


def pick_kernel(slots, saved, upstream, head, now, later, slot_values, sems):
    slot_copy = pltpu.make_async_copy(slots, slot_values, sems.at[6])
    copies = [
        pltpu.make_async_copy(upstream.at[0], now.at[0], sems.at[0]),
        pltpu.make_async_copy(head.at[0], later.at[2], sems.at[1]),
        pltpu.make_async_copy(head.at[1], later.at[3], sems.at[2]),
    ]
    slot_copy.start()
    for copy in copies:
        copy.start()
    slot_copy.wait()
    for tick, place in enumerate((now.at[1], later.at[0], later.at[1])):
        slot = jnp.clip(slot_values[0, tick], 0, 7)
        copies.append(pltpu.make_async_copy(saved.at[0, slot], place, sems.at[3 + tick]))
        copies[-1].start()
    for copy in copies:
        copy.wait()


LOADS = 4


def load_kernel(after, up, down, held_up, held_down, sems):
    copies = []
    for i in range(LOADS):
        rows = pl.ds(i * (512 // LOADS), 512 // LOADS)
        copies.append(pltpu.make_async_copy(up.at[0, rows], held_up.at[rows], sems.at[2 * i]))
        rows = pl.ds(i * (4096 // LOADS), 4096 // LOADS)
        copies.append(
            pltpu.make_async_copy(down.at[0, rows], held_down.at[rows], sems.at[2 * i + 1])
        )
    for copy in copies:
        copy.start()
    for copy in copies:
        copy.wait()


def emit(total, own, others):
    own[...] = total[:64]
    for by, other in enumerate(others):
        other[...] = total[64 * by + 64 : 64 * by + 128].astype(BF16)


PARTIAL = [((64, 512), F32)] + [((64, 512), BF16)] * 3
HIDDEN = [((256, PART), BF16)] * PARTS


def first_kernel(inputs, grad, up, down, own, o1, o2, o3, *refs):
    hiddens, maskeds = refs[:PARTS], refs[PARTS:]
    total = None
    for i in range(PARTS):
        for at in range(0, PART, WIDE):
            here = slice(at, at + WIDE)
            part = slice(i * PART + at, i * PART + at + WIDE)
            before = dot(inputs[...], up[:, part], ((1,), (0,)))
            hiddens[i][:, here] = jnp.maximum(before, 0.0).astype(BF16)
            raw = dot(grad[...], down[part, :], ((1,), (1,)))
            value = jnp.where(before > 0, raw, 0.0).astype(BF16)
            maskeds[i][:, here] = value
            term = dot(value, up[:, part], ((1,), (1,)))
            total = term if total is None else total + term
    emit(total, own, (o1, o2, o3))


def next_kernel(grad, *refs):
    hiddens, ups, downs = (refs[i * PARTS : (i + 1) * PARTS] for i in range(3))
    outs = refs[3 * PARTS :]
    masked = outs[4:]
    total = None
    for i in range(PARTS):
        for at in range(0, PART, WIDE):
            part = slice(at, at + WIDE)
            raw = dot(grad[...], downs[i][part, :], ((1,), (1,)))
            value = jnp.where(hiddens[i][:, part] > 0, raw, 0.0).astype(BF16)
            if masked:
                masked[i][:, part] = value
            term = dot(value, ups[i][:, part], ((1,), (1,)))
            total = term if total is None else total + term
    emit(total, outs[0], outs[1:4])


def sum_kernel(own, o1, o2, o3, *refs):
    total, rounded, swapped = refs[-3:]
    value = own[...]
    for other in (o1, o2, o3):
        value = value + other[...].astype(F32)
    total[...] = value
    value = value.astype(BF16)
    rounded[...] = value
    swapped[:32] = value[32:]
    swapped[32:] = value[:32]


def flags_at(delay, tick):
    return [(j + delay[0, j] <= tick).astype(F32) for j in range(tick)]


def up_kernel(tick, part_at, rate, delay, *refs):
    inputs, maskeds = refs[:tick], refs[tick : 2 * tick]
    following, first_up, *_, up, hidden = refs[2 * tick :]
    flags = flags_at(delay, tick)
    turned = jnp.concatenate(
        [(flag * x[...].astype(F32)).astype(BF16) for flag, x in zip(flags, inputs)], axis=0
    ).T
    for at in range(0, PART, CHUNK):
        part = slice(part_at + at, part_at + at + CHUNK)
        here = slice(at, at + CHUNK)
        masked = jnp.concatenate([m[:, here] for m in maskeds], axis=0)
        total = dot(turned, masked, ((1,), (0,)))
        value = (first_up[0, :, part].astype(F32) - rate * total).astype(BF16)
        up[:, here] = value
        before = dot(following[...], value, ((1,), (0,)))
        hidden[:, here] = jnp.maximum(before, 0.0).astype(BF16)


def down_kernel(tick, part_at, rate, delay, *refs):
    hiddens, grads = refs[:tick], refs[tick : 2 * tick]
    first_down, given, *_ = refs[2 * tick :]
    if tick == 1:
        down, passed = refs[-2:]
        passed[...] = given[...]
    else:
        down = refs[-1]
    flags = flags_at(delay, tick)
    scaled = jnp.concatenate(
        [(flag * g[...].astype(F32)).astype(BF16) for flag, g in zip(flags, grads)], axis=0
    )
    for at in range(0, PART, CHUNK):
        part = slice(part_at + at, part_at + at + CHUNK)
        here = slice(at, at + CHUNK)
        hidden = jnp.concatenate([h[:, here] for h in hiddens], axis=0)
        total = dot(hidden, scaled, ((0,), (0,)))
        down[here, :] = (first_down[0, part, :].astype(F32) - rate * total).astype(BF16)


def body(
    saved_inputs, microbatch_slot, staleness, up_weight, down_weight, upstream_grad, head_grad
):
    is_last = lax.axis_index("section") == lax.axis_size("section") - 1
    rates = learning_rates(256, 512, 32768)

    now, later = call(
        pick_kernel,
        [((2, 32, 512), BF16), ((4, 32, 512), BF16)],
        (IN_HBM,) * 4,
        0,
        "pick",
        microbatch_slot,
        saved_inputs,
        upstream_grad,
        head_grad,
        scratch=(pltpu.SMEM((1, 3), jnp.int32), pltpu.SemaphoreType.DMA((7,))),
    )
    now_pairs = pair_rows(now)
    first_up, first_down = call(
        load_kernel,
        [((512, 4096), BF16), ((4096, 512), BF16)],
        (IN_VMEM, IN_HBM, IN_HBM),
        2,
        "load",
        now_pairs,
        up_weight,
        down_weight,
        scratch=(pltpu.SemaphoreType.DMA((2 * LOADS,)),),
    )
    gathered = gather_blocks(now_pairs, 1)
    grad = gathered[0]
    inputs = [gathered[1]]
    pairs = pair_rows(later)
    head = [pairs[2], pairs[3]]

    hiddens, maskeds, grads, totals = [], [], [], []
    for tick in range(3):
        if tick == 0:
            outs = call(
                first_kernel,
                PARTIAL + HIDDEN * 2,
                (IN_VMEM,) * 4,
                3,
                "first",
                inputs[0],
                grad,
                first_up,
                first_down,
            )
            hiddens.append(outs[4 : 4 + PARTS])
            maskeds.append(outs[4 + PARTS :])
        else:
            outs = call(
                next_kernel,
                PARTIAL + HIDDEN * (tick < 2),
                (IN_VMEM,) * (1 + 3 * PARTS),
                2,
                "next",
                grad,
                *hiddens[tick],
                *ups,
                *downs,
            )
            maskeds.append(outs[4:])
        grads.append(grad)
        others = [along_y(outs[by], by) for by in (1, 2, 3)]
        if tick == 2:
            total = outs[0]
            for other in others:
                total = total + other.astype(F32)
            totals.append(total)
            break

        done = tick + 1

        def update_down(i, given, handed_on):
            return call(
                functools.partial(down_kernel, done, i * PART, rates[1]),
                [((PART, 512), BF16)] + [((2, 64, 512), BF16)] * handed_on,
                (IN_SMEM,) + (IN_VMEM,) * (2 * done + 1 + len(given)),
                done / PARTS,
                "down",
                staleness,
                *[h[i] for h in hiddens],
                *grads,
                down_weight,
                *given,
            )

        def update_up(i, given):
            return call(
                functools.partial(up_kernel, done, i * PART, rates[0]),
                [((512, PART), BF16), ((256, PART), BF16)],
                (IN_SMEM,) + (IN_VMEM,) * (2 * done + 2 + len(given)),
                (done + 1) / PARTS,
                "up",
                staleness,
                *inputs[:done],
                *[m[i] for m in maskeds],
                inputs[done],
                up_weight,
                *given,
            )

        def add(after):
            return call(
                sum_kernel,
                [((64, 512), F32), ((64, 512), BF16), ((64, 512), BF16)],
                (IN_VMEM,) * 5,
                0,
                "sum",
                outs[0],
                *others,
                after,
            )

        def shift(rounded, swapped):
            arrived = to_previous_section(rounded, 0).astype(F32) + to_previous_section(
                swapped, 1
            ).astype(F32)
            return jnp.where(is_last, head[tick], arrived.astype(BF16))

        if tick == 0:
            block = pairs[:2]
            first, block_1 = update_down(0, [block], True)
            total, rounded, swapped = add(block_1)
            arrived = shift(rounded, swapped)
            second, block_2 = update_down(1, [block, rounded], True)
            downs = [first, second]
            following = jnp.concatenate(
                [block, along_y(block_1, 1), along_y(block_2, 2), along_y(block_1, 3)], axis=1
            )
            inputs += [following[0], following[1]]
            both = [update_up(0, []), update_up(1, [])]
        else:
            both = [update_up(0, [])]
            total, rounded, swapped = add(both[0][1])
            arrived = shift(rounded, swapped)
            both.append(update_up(1, [rounded]))
            downs = [update_down(0, [rounded], False)[0], update_down(1, [arrived], False)[0]]
        totals.append(total)
        ups = [b[0] for b in both]
        hiddens.append([b[1] for b in both])
        grad = gather_blocks(arrived, 0)
    sent = jnp.stack([total[32:].astype(BF16) for total in totals])
    out = jnp.stack([total[:32] for total in totals]) + across_x(sent).astype(F32)
    return out.astype(BF16)[:, None]


def solution(mesh):
    placed = (
        P("section", None, "tensor", None),
        P("section", None),
        P("section", None),
        P("section", None, "tensor"),
        P("section", "tensor", None),
        P("section", "tensor", None),
        P(None, "tensor", None),
    )
    return jax.shard_map(
        body,
        mesh=mesh,
        in_specs=placed,
        out_specs=P(None, "section", "tensor", None),
        check_vma=False,
    )
```

```python
import functools
import math

import jax
import jax.numpy as jnp
from jax import lax
from jax.experimental import pallas as pl
from jax.experimental.pallas import tpu as pltpu
from jax.sharding import PartitionSpec as P

F32 = jnp.float32
BF16 = jnp.bfloat16
CHUNK = 512
WIDE = 1024
PART = 2048
PARTS = 4096 // PART


def learning_rates(total_rows, width, hidden_units):
    up_rate = 0.5 * math.sqrt(hidden_units) / (math.sqrt(total_rows) * width)
    down_rate = 0.5 / (math.sqrt(total_rows) * math.sqrt(hidden_units))
    return (up_rate, down_rate)


def across_x(value):
    return lax.ppermute(value, "tensor", [(i, i ^ 1) for i in range(8)])


def along_y(value, by):
    return lax.ppermute(value, "tensor", [(i, i ^ (2 * by)) for i in range(8)])


def to_previous_section(value, flip):
    sections = lax.axis_size("section")
    pairs = [
        (s * 8 + i, (s - 1) % sections * 8 + (i ^ flip))
        for s in range(sections)
        for i in range(8)
    ]
    return lax.ppermute(value, ("section", "tensor"), pairs)


def pair_rows(rows):
    return jnp.concatenate([rows, across_x(rows)], axis=1)


def gather_blocks(block, axis):
    return jnp.concatenate([block] + [along_y(block, by) for by in (1, 2, 3)], axis=axis)


def dot(a, b, dims):
    return lax.dot_general(a, b, (dims, ((), ())), preferred_element_type=F32)


IN_VMEM = pl.BlockSpec(memory_space=pltpu.VMEM)
IN_SMEM = pl.BlockSpec(memory_space=pltpu.SMEM)
IN_HBM = pl.BlockSpec(memory_space=pl.ANY)


def held(value):
    return pltpu.with_memory_space_constraint(value, pltpu.VMEM)


def left(value):
    return pltpu.with_memory_space_constraint(value, pltpu.HBM)


def call(kernel, outs, specs, matmuls, name, *operands, scratch=()):
    place = {id(IN_VMEM): held, id(IN_HBM): left}
    operands = [place.get(id(s), lambda x: x)(x) for x, s in zip(operands, specs)]
    return pl.pallas_call(
        kernel,
        out_shape=tuple(pltpu.VMEM(shape, dtype) for shape, dtype in outs),
        in_specs=list(specs),
        out_specs=(IN_VMEM,) * len(outs),
        scratch_shapes=list(scratch),
        compiler_params=pltpu.CompilerParams(vmem_limit_bytes=10 << 20),
        cost_estimate=pl.CostEstimate(
            flops=int(matmuls * 2 * 256 * 512 * 4096), bytes_accessed=0, transcendentals=0
        ),
        name=name,
    )(*operands)


def pick_kernel(slots, saved, upstream, head, now, later, slot_values, sems):
    slot_copy = pltpu.make_async_copy(slots, slot_values, sems.at[6])
    copies = [
        pltpu.make_async_copy(upstream.at[0], now.at[0], sems.at[0]),
        pltpu.make_async_copy(head.at[0], later.at[2], sems.at[1]),
        pltpu.make_async_copy(head.at[1], later.at[3], sems.at[2]),
    ]
    slot_copy.start()
    for copy in copies:
        copy.start()
    slot_copy.wait()
    for tick, place in enumerate((now.at[1], later.at[0], later.at[1])):
        slot = jnp.clip(slot_values[0, tick], 0, 7)
        copies.append(pltpu.make_async_copy(saved.at[0, slot], place, sems.at[3 + tick]))
        copies[-1].start()
    for copy in copies:
        copy.wait()


LOADS = 4


def load_kernel(after, up, down, held_up, held_down, sems):
    copies = []
    for i in range(LOADS):
        rows = pl.ds(i * (512 // LOADS), 512 // LOADS)
        copies.append(pltpu.make_async_copy(up.at[0, rows], held_up.at[rows], sems.at[2 * i]))
        rows = pl.ds(i * (4096 // LOADS), 4096 // LOADS)
        copies.append(
            pltpu.make_async_copy(down.at[0, rows], held_down.at[rows], sems.at[2 * i + 1])
        )
    for copy in copies:
        copy.start()
    for copy in copies:
        copy.wait()


def emit(total, own, others):
    own[...] = total[:64]
    for by, other in enumerate(others):
        other[...] = total[64 * by + 64 : 64 * by + 128].astype(BF16)


PARTIAL = [((64, 512), F32)] + [((64, 512), BF16)] * 3
HIDDEN = [((256, PART), BF16)] * PARTS


def first_kernel(inputs, grad, up, down, own, o1, o2, o3, *refs):
    hiddens, maskeds = refs[:PARTS], refs[PARTS:]
    total = None
    for i in range(PARTS):
        for at in range(0, PART, WIDE):
            here = slice(at, at + WIDE)
            part = slice(i * PART + at, i * PART + at + WIDE)
            before = dot(inputs[...], up[:, part], ((1,), (0,)))
            hiddens[i][:, here] = jnp.maximum(before, 0.0).astype(BF16)
            raw = dot(grad[...], down[part, :], ((1,), (1,)))
            value = jnp.where(before > 0, raw, 0.0).astype(BF16)
            maskeds[i][:, here] = value
            term = dot(value, up[:, part], ((1,), (1,)))
            total = term if total is None else total + term
    emit(total, own, (o1, o2, o3))


def next_kernel(grad, *refs):
    hiddens, ups, downs = (refs[i * PARTS : (i + 1) * PARTS] for i in range(3))
    outs = refs[3 * PARTS :]
    masked = outs[4:]
    total = None
    for i in range(PARTS):
        for at in range(0, PART, WIDE):
            part = slice(at, at + WIDE)
            raw = dot(grad[...], downs[i][part, :], ((1,), (1,)))
            value = jnp.where(hiddens[i][:, part] > 0, raw, 0.0).astype(BF16)
            if masked:
                masked[i][:, part] = value
            term = dot(value, ups[i][:, part], ((1,), (1,)))
            total = term if total is None else total + term
    emit(total, outs[0], outs[1:4])


def sum_kernel(own, o1, o2, o3, *refs):
    total, rounded, swapped = refs[-3:]
    value = own[...]
    for other in (o1, o2, o3):
        value = value + other[...].astype(F32)
    total[...] = value
    value = value.astype(BF16)
    rounded[...] = value
    swapped[:32] = value[32:]
    swapped[32:] = value[:32]


def flags_at(delay, tick):
    return [(j + delay[0, j] <= tick).astype(F32) for j in range(tick)]


def up_kernel(tick, part_at, rate, delay, *refs):
    inputs, maskeds = refs[:tick], refs[tick : 2 * tick]
    following, first_up, *_, up, hidden = refs[2 * tick :]
    flags = flags_at(delay, tick)
    turned = jnp.concatenate(
        [(flag * x[...].astype(F32)).astype(BF16) for flag, x in zip(flags, inputs)], axis=0
    ).T
    for at in range(0, PART, CHUNK):
        part = slice(part_at + at, part_at + at + CHUNK)
        here = slice(at, at + CHUNK)
        masked = jnp.concatenate([m[:, here] for m in maskeds], axis=0)
        total = dot(turned, masked, ((1,), (0,)))
        value = (first_up[0, :, part].astype(F32) - rate * total).astype(BF16)
        up[:, here] = value
        before = dot(following[...], value, ((1,), (0,)))
        hidden[:, here] = jnp.maximum(before, 0.0).astype(BF16)


def down_kernel(tick, part_at, rate, delay, *refs):
    hiddens, grads = refs[:tick], refs[tick : 2 * tick]
    first_down, given, *_ = refs[2 * tick :]
    if tick == 1:
        down, passed = refs[-2:]
        passed[...] = given[...]
    else:
        down = refs[-1]
    flags = flags_at(delay, tick)
    scaled = jnp.concatenate(
        [(flag * g[...].astype(F32)).astype(BF16) for flag, g in zip(flags, grads)], axis=0
    )
    for at in range(0, PART, CHUNK):
        part = slice(part_at + at, part_at + at + CHUNK)
        here = slice(at, at + CHUNK)
        hidden = jnp.concatenate([h[:, here] for h in hiddens], axis=0)
        total = dot(hidden, scaled, ((0,), (0,)))
        down[here, :] = (first_down[0, part, :].astype(F32) - rate * total).astype(BF16)


def body(
    saved_inputs, microbatch_slot, staleness, up_weight, down_weight, upstream_grad, head_grad
):
    is_last = lax.axis_index("section") == lax.axis_size("section") - 1
    rates = learning_rates(256, 512, 32768)

    now, later = call(
        pick_kernel,
        [((2, 32, 512), BF16), ((4, 32, 512), BF16)],
        (IN_HBM,) * 4,
        0,
        "pick",
        microbatch_slot,
        saved_inputs,
        upstream_grad,
        head_grad,
        scratch=(pltpu.SMEM((1, 3), jnp.int32), pltpu.SemaphoreType.DMA((7,))),
    )
    now_pairs = pair_rows(now)
    first_up, first_down = call(
        load_kernel,
        [((512, 4096), BF16), ((4096, 512), BF16)],
        (IN_VMEM, IN_HBM, IN_HBM),
        2,
        "load",
        now_pairs,
        up_weight,
        down_weight,
        scratch=(pltpu.SemaphoreType.DMA((2 * LOADS,)),),
    )
    gathered = gather_blocks(now_pairs, 1)
    grad = gathered[0]
    inputs = [gathered[1]]
    pairs = pair_rows(later)
    head = [pairs[2], pairs[3]]

    hiddens, maskeds, grads, totals = [], [], [], []
    for tick in range(3):
        if tick == 0:
            outs = call(
                first_kernel,
                PARTIAL + HIDDEN * 2,
                (IN_VMEM,) * 4,
                3,
                "first",
                inputs[0],
                grad,
                first_up,
                first_down,
            )
            hiddens.append(outs[4 : 4 + PARTS])
            maskeds.append(outs[4 + PARTS :])
        else:
            outs = call(
                next_kernel,
                PARTIAL + HIDDEN * (tick < 2),
                (IN_VMEM,) * (1 + 3 * PARTS),
                2,
                "next",
                grad,
                *hiddens[tick],
                *ups,
                *downs,
            )
            maskeds.append(outs[4:])
        grads.append(grad)
        others = [along_y(outs[by], by) for by in (1, 2, 3)]
        if tick == 2:
            total = outs[0]
            for other in [others[i] for i in (1, 2, 0)]:
                total = total + other.astype(F32)
            totals.append(total)
            break

        done = tick + 1

        def update_down(i, given, handed_on):
            return call(
                functools.partial(down_kernel, done, i * PART, rates[1]),
                [((PART, 512), BF16)] + [((2, 64, 512), BF16)] * handed_on,
                (IN_SMEM,) + (IN_VMEM,) * (2 * done + 1 + len(given)),
                done / PARTS,
                "down",
                staleness,
                *[h[i] for h in hiddens],
                *grads,
                down_weight,
                *given,
            )

        def update_up(i, given):
            return call(
                functools.partial(up_kernel, done, i * PART, rates[0]),
                [((512, PART), BF16), ((256, PART), BF16)],
                (IN_SMEM,) + (IN_VMEM,) * (2 * done + 2 + len(given)),
                (done + 1) / PARTS,
                "up",
                staleness,
                *inputs[:done],
                *[m[i] for m in maskeds],
                inputs[done],
                up_weight,
                *given,
            )

        def add(after):
            return call(
                sum_kernel,
                [((64, 512), F32), ((64, 512), BF16), ((64, 512), BF16)],
                (IN_VMEM,) * 5,
                0,
                "sum",
                outs[0],
                *[others[i] for i in (1, 2, 0)],
                after,
            )

        def shift(rounded, swapped):
            arrived = to_previous_section(rounded, 0).astype(F32) + to_previous_section(
                swapped, 1
            ).astype(F32)
            return jnp.where(is_last, head[tick], arrived.astype(BF16))

        if tick == 0:
            block = pairs[:2]
            first, block_1 = update_down(0, [block], True)
            total, rounded, swapped = add(block_1)
            arrived = shift(rounded, swapped)
            second, block_2 = update_down(1, [block, rounded], True)
            downs = [first, second]
            following = jnp.concatenate(
                [block, along_y(block_1, 1), along_y(block_2, 2), along_y(block_1, 3)], axis=1
            )
            inputs += [following[0], following[1]]
            both = [update_up(0, []), update_up(1, [])]
        else:
            both = [update_up(0, [])]
            total, rounded, swapped = add(both[0][1])
            arrived = shift(rounded, swapped)
            both.append(update_up(1, [rounded]))
            downs = [update_down(0, [rounded], False)[0], update_down(1, [arrived], False)[0]]
        totals.append(total)
        ups = [b[0] for b in both]
        hiddens.append([b[1] for b in both])
        grad = gather_blocks(arrived, 0)
    sent = jnp.stack([total[32:].astype(BF16) for total in totals])
    out = jnp.stack([total[:32] for total in totals]) + across_x(sent).astype(F32)
    return out.astype(BF16)[:, None]


def solution(mesh):
    placed = (
        P("section", None, "tensor", None),
        P("section", None),
        P("section", None),
        P("section", None, "tensor"),
        P("section", "tensor", None),
        P("section", "tensor", None),
        P(None, "tensor", None),
    )
    return jax.shard_map(
        body,
        mesh=mesh,
        in_specs=placed,
        out_specs=P(None, "section", "tensor", None),
        check_vma=False,
    )
```

```python
import functools
import math

import jax
import jax.numpy as jnp
from jax import lax
from jax.experimental import pallas as pl
from jax.experimental.pallas import tpu as pltpu
from jax.sharding import PartitionSpec as P

F32 = jnp.float32
BF16 = jnp.bfloat16
CHUNK = 512
WIDE = 1024
PART = 2048
PARTS = 4096 // PART


def learning_rates(total_rows, width, hidden_units):
    up_rate = 0.5 * math.sqrt(hidden_units) / (math.sqrt(total_rows) * width)
    down_rate = 0.5 / (math.sqrt(total_rows) * math.sqrt(hidden_units))
    return (up_rate, down_rate)


STEPS = (0, 1, 3, 2)


def across_x(value):
    return lax.ppermute(value, "tensor", [(i, i ^ 1) for i in range(8)])


def along_y(value, by):
    return lax.ppermute(value, "tensor", [(i, i ^ (2 * by)) for i in range(8)])


def to_previous_section(value, flip):
    sections = lax.axis_size("section")
    pairs = [
        (s * 8 + i, (s - 1) % sections * 8 + (i ^ flip))
        for s in range(sections)
        for i in range(8)
    ]
    return lax.ppermute(value, ("section", "tensor"), pairs)


def pair_rows(rows):
    return jnp.concatenate([rows, across_x(rows)], axis=1)


def gather_blocks(block, axis):
    return jnp.concatenate([block] + [along_y(block, step) for step in STEPS[1:]], axis=axis)


def dot(a, b, dims):
    return lax.dot_general(a, b, (dims, ((), ())), preferred_element_type=F32)


IN_VMEM = pl.BlockSpec(memory_space=pltpu.VMEM)
IN_SMEM = pl.BlockSpec(memory_space=pltpu.SMEM)
IN_HBM = pl.BlockSpec(memory_space=pl.ANY)


def held(value):
    return pltpu.with_memory_space_constraint(value, pltpu.VMEM)


def left(value):
    return pltpu.with_memory_space_constraint(value, pltpu.HBM)


def call(kernel, outs, specs, matmuls, name, *operands, scratch=()):
    place = {id(IN_VMEM): held, id(IN_HBM): left}
    operands = [place.get(id(s), lambda x: x)(x) for x, s in zip(operands, specs)]
    return pl.pallas_call(
        kernel,
        out_shape=tuple(pltpu.VMEM(shape, dtype) for shape, dtype in outs),
        in_specs=list(specs),
        out_specs=(IN_VMEM,) * len(outs),
        scratch_shapes=list(scratch),
        compiler_params=pltpu.CompilerParams(vmem_limit_bytes=10 << 20),
        cost_estimate=pl.CostEstimate(
            flops=int(matmuls * 2 * 256 * 512 * 4096), bytes_accessed=0, transcendentals=0
        ),
        name=name,
    )(*operands)


def pick_kernel(slots, saved, upstream, head, now, later, slot_values, sems):
    slot_copy = pltpu.make_async_copy(slots, slot_values, sems.at[6])
    copies = [
        pltpu.make_async_copy(upstream.at[0], now.at[0], sems.at[0]),
        pltpu.make_async_copy(head.at[0], later.at[2], sems.at[1]),
        pltpu.make_async_copy(head.at[1], later.at[3], sems.at[2]),
    ]
    slot_copy.start()
    for copy in copies:
        copy.start()
    slot_copy.wait()
    for tick, place in enumerate((now.at[1], later.at[0], later.at[1])):
        slot = jnp.clip(slot_values[0, tick], 0, 7)
        copies.append(pltpu.make_async_copy(saved.at[0, slot], place, sems.at[3 + tick]))
        copies[-1].start()
    for copy in copies:
        copy.wait()


LOADS = 4


def load_kernel(after, up, down, held_up, held_down, sems):
    copies = []
    for i in range(LOADS):
        rows = pl.ds(i * (512 // LOADS), 512 // LOADS)
        copies.append(pltpu.make_async_copy(up.at[0, rows], held_up.at[rows], sems.at[2 * i]))
        rows = pl.ds(i * (4096 // LOADS), 4096 // LOADS)
        copies.append(
            pltpu.make_async_copy(down.at[0, rows], held_down.at[rows], sems.at[2 * i + 1])
        )
    for copy in copies:
        copy.start()
    for copy in copies:
        copy.wait()


def emit(total, own, others):
    own[...] = total[:64]
    for by, other in enumerate(others):
        other[...] = total[64 * by + 64 : 64 * by + 128].astype(BF16)


PARTIAL = [((64, 512), F32)] + [((64, 512), BF16)] * 3
HIDDEN = [((256, PART), BF16)] * PARTS


def first_kernel(inputs, grad, up, down, own, o1, o2, o3, *refs):
    hiddens, maskeds = refs[:PARTS], refs[PARTS:]
    total = None
    for i in range(PARTS):
        for at in range(0, PART, WIDE):
            here = slice(at, at + WIDE)
            part = slice(i * PART + at, i * PART + at + WIDE)
            before = dot(inputs[...], up[:, part], ((1,), (0,)))
            hiddens[i][:, here] = jnp.maximum(before, 0.0).astype(BF16)
            raw = dot(grad[...], down[part, :], ((1,), (1,)))
            value = jnp.where(before > 0, raw, 0.0).astype(BF16)
            maskeds[i][:, here] = value
            term = dot(value, up[:, part], ((1,), (1,)))
            total = term if total is None else total + term
    emit(total, own, (o1, o2, o3))


def next_kernel(grad, *refs):
    hiddens, ups, downs = (refs[i * PARTS : (i + 1) * PARTS] for i in range(3))
    outs = refs[3 * PARTS :]
    masked = outs[4:]
    total = None
    for i in range(PARTS):
        for at in range(0, PART, WIDE):
            part = slice(at, at + WIDE)
            raw = dot(grad[...], downs[i][part, :], ((1,), (1,)))
            value = jnp.where(hiddens[i][:, part] > 0, raw, 0.0).astype(BF16)
            if masked:
                masked[i][:, part] = value
            term = dot(value, ups[i][:, part], ((1,), (1,)))
            total = term if total is None else total + term
    emit(total, outs[0], outs[1:4])


def sum_kernel(own, o1, o2, o3, *refs):
    total, rounded, swapped = refs[-3:]
    value = own[...]
    for other in (o1, o2, o3):
        value = value + other[...].astype(F32)
    total[...] = value
    value = value.astype(BF16)
    rounded[...] = value
    swapped[:32] = value[32:]
    swapped[32:] = value[:32]


def flags_at(delay, tick):
    return [(j + delay[0, j] <= tick).astype(F32) for j in range(tick)]


def up_kernel(tick, part_at, rate, delay, *refs):
    inputs, maskeds = refs[:tick], refs[tick : 2 * tick]
    following, first_up, *_, up, hidden = refs[2 * tick :]
    flags = flags_at(delay, tick)
    turned = jnp.concatenate(
        [(flag * x[...].astype(F32)).astype(BF16) for flag, x in zip(flags, inputs)], axis=0
    ).T
    for at in range(0, PART, CHUNK):
        part = slice(part_at + at, part_at + at + CHUNK)
        here = slice(at, at + CHUNK)
        masked = jnp.concatenate([m[:, here] for m in maskeds], axis=0)
        total = dot(turned, masked, ((1,), (0,)))
        value = (first_up[0, :, part].astype(F32) - rate * total).astype(BF16)
        up[:, here] = value
        before = dot(following[...], value, ((1,), (0,)))
        hidden[:, here] = jnp.maximum(before, 0.0).astype(BF16)


def down_kernel(tick, part_at, rate, delay, *refs):
    hiddens, grads = refs[:tick], refs[tick : 2 * tick]
    first_down, given, *_ = refs[2 * tick :]
    if tick == 1:
        down, passed = refs[-2:]
        passed[...] = given[...]
    else:
        down = refs[-1]
    flags = flags_at(delay, tick)
    scaled = jnp.concatenate(
        [(flag * g[...].astype(F32)).astype(BF16) for flag, g in zip(flags, grads)], axis=0
    )
    for at in range(0, PART, CHUNK):
        part = slice(part_at + at, part_at + at + CHUNK)
        here = slice(at, at + CHUNK)
        hidden = jnp.concatenate([h[:, here] for h in hiddens], axis=0)
        total = dot(hidden, scaled, ((0,), (0,)))
        down[here, :] = (first_down[0, part, :].astype(F32) - rate * total).astype(BF16)


def body(
    saved_inputs, microbatch_slot, staleness, up_weight, down_weight, upstream_grad, head_grad
):
    is_last = lax.axis_index("section") == lax.axis_size("section") - 1
    rates = learning_rates(256, 512, 32768)

    now, later = call(
        pick_kernel,
        [((2, 32, 512), BF16), ((4, 32, 512), BF16)],
        (IN_HBM,) * 4,
        0,
        "pick",
        microbatch_slot,
        saved_inputs,
        upstream_grad,
        head_grad,
        scratch=(pltpu.SMEM((1, 3), jnp.int32), pltpu.SemaphoreType.DMA((7,))),
    )
    now_pairs = pair_rows(now)
    first_up, first_down = call(
        load_kernel,
        [((512, 4096), BF16), ((4096, 512), BF16)],
        (IN_VMEM, IN_HBM, IN_HBM),
        2,
        "load",
        now_pairs,
        up_weight,
        down_weight,
        scratch=(pltpu.SemaphoreType.DMA((2 * LOADS,)),),
    )
    gathered = gather_blocks(now_pairs, 1)
    grad = gathered[0]
    inputs = [gathered[1]]
    pairs = pair_rows(later)
    head = [pairs[2], pairs[3]]

    hiddens, maskeds, grads, totals = [], [], [], []
    for tick in range(3):
        if tick == 0:
            outs = call(
                first_kernel,
                PARTIAL + HIDDEN * 2,
                (IN_VMEM,) * 4,
                3,
                "first",
                inputs[0],
                grad,
                first_up,
                first_down,
            )
            hiddens.append(outs[4 : 4 + PARTS])
            maskeds.append(outs[4 + PARTS :])
        else:
            outs = call(
                next_kernel,
                PARTIAL + HIDDEN * (tick < 2),
                (IN_VMEM,) * (1 + 3 * PARTS),
                2,
                "next",
                grad,
                *hiddens[tick],
                *ups,
                *downs,
            )
            maskeds.append(outs[4:])
        grads.append(grad)
        others = [along_y(outs[j], STEPS[j]) for j in (1, 2, 3)]
        if tick == 2:
            total = outs[0]
            for other in others[::-1]:
                total = total + other.astype(F32)
            totals.append(total)
            break

        done = tick + 1

        def update_down(i, given, handed_on):
            return call(
                functools.partial(down_kernel, done, i * PART, rates[1]),
                [((PART, 512), BF16)] + [((2, 64, 512), BF16)] * handed_on,
                (IN_SMEM,) + (IN_VMEM,) * (2 * done + 1 + len(given)),
                done / PARTS,
                "down",
                staleness,
                *[h[i] for h in hiddens],
                *grads,
                down_weight,
                *given,
            )

        def update_up(i, given):
            return call(
                functools.partial(up_kernel, done, i * PART, rates[0]),
                [((512, PART), BF16), ((256, PART), BF16)],
                (IN_SMEM,) + (IN_VMEM,) * (2 * done + 2 + len(given)),
                (done + 1) / PARTS,
                "up",
                staleness,
                *inputs[:done],
                *[m[i] for m in maskeds],
                inputs[done],
                up_weight,
                *given,
            )

        def add(after):
            return call(
                sum_kernel,
                [((64, 512), F32), ((64, 512), BF16), ((64, 512), BF16)],
                (IN_VMEM,) * 5,
                0,
                "sum",
                outs[0],
                *others[::-1],
                after,
            )

        def shift(rounded, swapped):
            arrived = to_previous_section(rounded, 0).astype(F32) + to_previous_section(
                swapped, 1
            ).astype(F32)
            return jnp.where(is_last, head[tick], arrived.astype(BF16))

        if tick == 0:
            block = pairs[:2]
            first, block_1 = update_down(0, [block], True)
            total, rounded, swapped = add(block_1)
            arrived = shift(rounded, swapped)
            second, block_2 = update_down(1, [block, rounded], True)
            downs = [first, second]
            following = jnp.concatenate(
                [block, along_y(block_1, 1), along_y(block_1, 3), along_y(block_2, 2)], axis=1
            )
            inputs += [following[0], following[1]]
            both = [update_up(0, []), update_up(1, [])]
        else:
            both = [update_up(0, [])]
            total, rounded, swapped = add(both[0][1])
            arrived = shift(rounded, swapped)
            both.append(update_up(1, [rounded]))
            downs = [update_down(0, [rounded], False)[0], update_down(1, [arrived], False)[0]]
        totals.append(total)
        ups = [b[0] for b in both]
        hiddens.append([b[1] for b in both])
        grad = gather_blocks(arrived, 0)
    sent = jnp.stack([total[32:].astype(BF16) for total in totals])
    out = jnp.stack([total[:32] for total in totals]) + across_x(sent).astype(F32)
    return out.astype(BF16)[:, None]


def solution(mesh):
    placed = (
        P("section", None, "tensor", None),
        P("section", None),
        P("section", None),
        P("section", None, "tensor"),
        P("section", "tensor", None),
        P("section", "tensor", None),
        P(None, "tensor", None),
    )
    return jax.shard_map(
        body,
        mesh=mesh,
        in_specs=placed,
        out_specs=P(None, "section", "tensor", None),
        check_vma=False,
    )
```
